512 devices in a mesh: clus: 8 (over y, core), blk: 64 (over z, x).
Axes of the slice: x: 4, y: 4, z: 16, core: 2. Of those that a mesh axis runs over, the one named last changes fastest.
Arguments:
- embeddings: bfloat16 [262144, 1024], P(('clus', 'blk')), may hold values from -120 to 120
- cluster_sizes: int32 [170], replicated, may hold values from 1 to 5, 512 in all
Outputs:
- best_score: float32 [262144], P(('clus', 'blk'))
- soft_count: float32 [262144], P(('clus', 'blk'))
The draws below stay inside these ranges and needn't reach their ends.
All inputs are finite; a program needn't handle non-finite values.
Results may differ from the reference program's by a relative error of at most 0.001.
Values may be sent and summed in bfloat16 or wider, within the bound.
No kernel may reach another device: no remote copies, remote signals or barrier semaphores. Data moves between devices by JAX's collectives and lax.ppermute only.
A program may use at most 64 MiB of HBM per device.

```python
import math
import jax
import jax.numpy as jnp
import numpy as np
from jax import lax

D = 1024
ROWS = 512
MOST = 5
CLUSTERS = 170
ROWS_ALL = 262144
N_CLUS = 8
N_BLK = 64
DEVICES = 512


def draw_embeddings(key, part):
    key = jax.random.fold_in(key, 7)
    key_proto, key_pick, key_strength, key_jitter = jax.random.split(key, 4)
    pool_rows = 8 * ROWS
    protos = jnp.clip(jax.random.normal(key_proto, (pool_rows, D), jnp.float32), -4.0, 4.0)
    picked = jax.random.randint(key_pick, (ROWS_ALL,), 0, pool_rows)
    strength = jnp.exp(jax.random.uniform(key_strength, (ROWS_ALL, 1), jnp.float32, math.log(0.3), math.log(2.0)))
    jitter = jnp.clip(jax.random.normal(key_jitter, (ROWS_ALL, D), jnp.float32), -4.0, 4.0)
    return (strength * protos[picked] + jitter).astype(jnp.bfloat16)


def split_up(amount, total, most, skew):
    weights = [(1 << 20) // math.isqrt(standing ** skew) + 1 for standing in range(2, amount + 1)]
    rest, holding = total - most - (amount - 1), [1] * (amount - 1)
    while rest > 0:
        free = [i for i in range(amount - 1) if holding[i] < most]
        whole, budget = sum([weights[i] for i in free]), rest
        for i in free:
            more = min(most - holding[i], max(1, budget * weights[i] // whole), rest)
            holding[i] = holding[i] + more
            rest = rest - more
    return np.array([most] + holding)


def ragged(key, number_of, total, most, skew):
    if number_of == 2:
        one = jax.random.randint(key, (), max(1, total - most), min(most, total - 1) + 1)
        return jnp.stack([one, total - one])
    lengths = jnp.asarray(split_up(number_of, total, most, skew), jnp.int32)
    twos = (number_of - 1) // 2
    source_of, taker = lengths[1:1 + 2 * twos:2], lengths[2:2 + 2 * twos:2]
    slack = jnp.minimum(source_of - 1, most - taker)
    shifted = jax.random.randint(jax.random.fold_in(key, 1), (twos,), 0, 1 << 20) % (slack + 1)
    lengths = lengths.at[1:1 + 2 * twos:2].set(source_of - shifted).at[2:2 + 2 * twos:2].set(taker + shifted)
    return lengths[jax.random.permutation(jax.random.fold_in(key, 2), number_of)]


def setup_inputs(seed: int = 0) -> dict:
    splits = jax.random.split(jax.random.key(seed), 3)
    embeddings = draw_embeddings(jax.random.fold_in(splits[2], 71), 0)
    cluster_sizes = ragged(splits[1], CLUSTERS, DEVICES, MOST, 2).astype(jnp.int32)
    return dict(embeddings=embeddings, cluster_sizes=cluster_sizes)


epsilon = 1e-06
threshold = 0.5
sharpness = 20.0
floor_value = -2.0

def unitize(values):
    widened = values.astype(jnp.float32)
    factor = lax.rsqrt(lax.optimization_barrier(jnp.mean(widened * widened, axis=-1, keepdims=True)) + epsilon) * (1.0 / math.sqrt(values.shape[-1]))
    return (widened * factor).astype(jnp.bfloat16)

def block_stats(mine_rows, other_rows):
    scores = lax.dot_general(mine_rows, other_rows, (((1,), (1,)), ((), ())), preferred_element_type=jnp.float32)
    closeness = jax.nn.sigmoid(sharpness * (scores - threshold))
    return (lax.optimization_barrier(jnp.max(scores, axis=1)), lax.optimization_barrier(jnp.sum(closeness, axis=1)), lax.optimization_barrier(jnp.max(scores, axis=0)), lax.optimization_barrier(jnp.sum(closeness, axis=0)))

def empty_stats(length):
    lowest = jnp.full((length,), floor_value, jnp.float32)
    nought = jnp.zeros((length,), jnp.float32)
    return (lowest, nought, lowest, nought)

def diag_stats(mine_rows):
    scores = lax.dot_general(mine_rows, mine_rows, (((1,), (1,)), ((), ())), preferred_element_type=jnp.float32)
    length = mine_rows.shape[0]
    self_pair = lax.broadcasted_iota(jnp.int32, (length, length), 0) == lax.broadcasted_iota(jnp.int32, (length, length), 1)
    closeness = jnp.where(self_pair, jnp.float32(0.0), jax.nn.sigmoid(sharpness * (scores - threshold)))
    masked = jnp.where(self_pair, jnp.float32(floor_value), scores)
    return (lax.optimization_barrier(jnp.max(masked, axis=1)), lax.optimization_barrier(jnp.sum(closeness, axis=1)))

def reference(embeddings, cluster_sizes):
    holders = N_CLUS * N_BLK
    normed = unitize(embeddings).reshape(holders, ROWS, D)
    cluster_end = jnp.cumsum(cluster_sizes).astype(jnp.int32)
    slots = jnp.arange(holders, dtype=jnp.int32)
    cluster_of = lax.optimization_barrier(jnp.sum((cluster_end[None, :] <= slots[:, None]).astype(jnp.int32), axis=1))
    best_start, count_start = lax.map(diag_stats, normed)

    def visit(holder, totals):
        best_score, soft_count = totals
        for distance in range(1, MOST):
            partner = jnp.maximum(holder - distance, 0).astype(jnp.int32)
            usable = (holder - distance >= 0) & (cluster_of[partner] == cluster_of[holder])
            mine_rows = normed[holder]
            other_rows = normed[partner]
            row_best, row_count, col_best, col_count = lax.cond(usable, lambda: block_stats(mine_rows, other_rows), lambda: empty_stats(ROWS))
            best_score = best_score.at[holder].max(row_best)
            soft_count = soft_count.at[holder].add(row_count)
            best_score = best_score.at[partner].max(col_best)
            soft_count = soft_count.at[partner].add(col_count)
        return (best_score, soft_count)
    best_score, soft_count = lax.fori_loop(0, holders, visit, (best_start, count_start))
    return (best_score.reshape(-1), soft_count.reshape(-1))
```

```python
import math

import jax
import jax.numpy as jnp
from jax import lax
from jax.experimental import pallas as pl
from jax.experimental.pallas import tpu as pltpu
from jax.sharding import PartitionSpec as P

MOST = 5
AXES = ("clus", "blk")
RING = 4

epsilon = 1e-06
threshold = 0.5
sharpness = 20.0
floor_value = -2.0

OWN, FIRST, SECOND, BELOW, EDGE = range(5)


def upper_source(p):
    return p - 1 if p % RING else p + RING - 1


def lower_source(p):
    return p + 1 if p % RING else p + RING + 1


def routes(total, line):
    below, first, second, edge, up, down = [], [], [], [], [], []
    for p in range(total):
        if p >= RING:
            below.append((p - RING, p))
        odd_line = (p // line) % 2
        u, d = upper_source(p), lower_source(p)
        up.append((u, p))
        (second if odd_line else first).append((u, p))
        if d < total:
            down.append((d, p))
            if d // line != p // line:
                edge.append((d, p))
            else:
                (first if odd_line else second).append((d, p))
    return below, first, second, edge, up, down


def inverse(route):
    return [(b, a) for a, b in route]


def unitize(values):
    widened = values.astype(jnp.float32)
    factor = lax.rsqrt(jnp.mean(widened * widened, axis=-1, keepdims=True) + epsilon) * (
        1.0 / math.sqrt(values.shape[-1])
    )
    return (widened * factor).astype(jnp.bfloat16)


def closeness_of(scores):
    return 1.0 / (1.0 + jnp.exp(-sharpness * (scores - threshold)))


def fold_rows(part, op):
    width = part.shape[1]
    folded = part[:, :128]
    for k in range(1, width // 128):
        folded = op(folded, part[:, k * 128 : (k + 1) * 128])
    flipped = folded.T
    return flipped


def diag_kernel(x_ref, out_ref):
    rows = x_ref.shape[0]
    step = 128
    for r in range(rows // step):
        scores = lax.dot_general(
            x_ref[r * step : (r + 1) * step, :],
            x_ref[...],
            (((1,), (1,)), ((), ())),
            preferred_element_type=jnp.float32,
        )
        self_pair = (
            lax.broadcasted_iota(jnp.int32, scores.shape, 0) + r * step
            == lax.broadcasted_iota(jnp.int32, scores.shape, 1)
        )
        near = jnp.where(self_pair, 0.0, closeness_of(scores))
        high = jnp.where(self_pair, floor_value, scores)
        span = slice(r * step, (r + 1) * step)
        out_ref[0:1, span] = jnp.max(fold_rows(high, jnp.maximum), axis=0, keepdims=True)
        out_ref[1:2, span] = jnp.sum(fold_rows(near, jnp.add), axis=0, keepdims=True)


def pair_kernel(table_ref, x_ref, a_ref, b_ref, z_ref, e_ref, own_ref, ox_ref, ou_ref, od_ref, oz_ref, slabs, best, count):
    rows = x_ref.shape[0]
    step = 128
    slabs[OWN] = x_ref[...]
    slabs[FIRST] = a_ref[...]
    slabs[SECOND] = b_ref[...]
    slabs[BELOW] = z_ref[...]
    slabs[EDGE] = e_ref[...]
    best[...] = jnp.full(best.shape, floor_value, jnp.float32)
    count[...] = jnp.zeros(count.shape, jnp.float32)

    def one(k, carry):
        i, j = table_ref[2 * k + 1], table_ref[2 * k + 2]

        for r in range(rows // step):
            scores = lax.dot_general(
                slabs[i, r * step : (r + 1) * step, :],
                slabs[j],
                (((1,), (1,)), ((), ())),
                preferred_element_type=jnp.float32,
            )
            near = closeness_of(scores)
            span = slice(r * step, (r + 1) * step)
            tall = (step // 8, 8, rows)
            best[j] = jnp.maximum(best[j], jnp.max(scores.reshape(tall), axis=0))
            count[j] = count[j] + jnp.sum(near.reshape(tall), axis=0)
            high_t = fold_rows(scores, jnp.maximum).reshape(16, 8, step)
            near_t = fold_rows(near, jnp.add).reshape(16, 8, step)
            best[i, :, span] = jnp.maximum(best[i, :, span], jnp.max(high_t, axis=0))
            count[i, :, span] = count[i, :, span] + jnp.sum(near_t, axis=0)
        return carry

    lax.fori_loop(0, table_ref[0], one, 0)

    def emit(ref, slot):
        ref[0:1, :] = jnp.max(best[slot], axis=0, keepdims=True)
        ref[1:2, :] = jnp.sum(count[slot], axis=0, keepdims=True)

    iu, idn = table_ref[11], table_ref[12]
    ox_ref[0:1, :] = jnp.maximum(own_ref[0:1, :], jnp.max(best[OWN], axis=0, keepdims=True))
    ox_ref[1:2, :] = own_ref[1:2, :] + jnp.sum(count[OWN], axis=0, keepdims=True)
    emit(ou_ref, iu)
    emit(od_ref, idn)
    emit(oz_ref, BELOW)


VMEM = pl.BlockSpec(memory_space=pltpu.VMEM)


def pair_stats(table, own_slab, first, second, below, edge, own):
    rows, width = own_slab.shape
    stat = jax.ShapeDtypeStruct((2, rows), jnp.float32)
    return pl.pallas_call(
        pair_kernel,
        in_specs=[pl.BlockSpec(memory_space=pltpu.SMEM)] + [VMEM] * 6,
        out_specs=[VMEM] * 4,
        out_shape=[stat] * 4,
        scratch_shapes=[
            pltpu.VMEM((5, rows, width), jnp.bfloat16),
            pltpu.VMEM((5, 8, rows), jnp.float32),
            pltpu.VMEM((5, 8, rows), jnp.float32),
        ],
        compiler_params=pltpu.CompilerParams(vmem_limit_bytes=40 * 1024 * 1024),
        cost_estimate=pl.CostEstimate(flops=3 * 2 * rows * rows * width, bytes_accessed=5 * rows * width * 2, transcendentals=0),
    )(table, own_slab, first, second, below, edge, own)


def diag_stats(own_slab):
    rows, width = own_slab.shape
    return pl.pallas_call(
        diag_kernel,
        in_specs=[VMEM],
        out_specs=VMEM,
        out_shape=jax.ShapeDtypeStruct((2, rows), jnp.float32),
        compiler_params=pltpu.CompilerParams(vmem_limit_bytes=20 * 1024 * 1024),
        cost_estimate=pl.CostEstimate(flops=2 * rows * rows * width, bytes_accessed=rows * width * 2, transcendentals=0),
    )(own_slab)


def pair_table(cluster_sizes, line, total):
    p = lax.axis_index(AXES)
    x = p % RING
    odd_line = (p // line) % 2
    cluster_end = jnp.cumsum(cluster_sizes)

    def cluster_of(q):
        return jnp.sum((cluster_end <= q).astype(jnp.int32))

    mine = cluster_of(p)
    qu = jnp.where(x == 0, p + RING - 1, p - 1)
    qd = jnp.where(x == 0, p + RING + 1, p + 1)
    qz = p - RING
    cu, cd, cz = cluster_of(qu), cluster_of(qd), cluster_of(qz)
    has_d = qd < total
    has_z = qz >= 0
    iu = jnp.where(odd_line == 1, SECOND, FIRST)
    idn = jnp.where(qd // line != p // line, EDGE, jnp.where(odd_line == 1, FIRST, SECOND))
    wanted = [
        (cu == mine, OWN, iu),
        ((cd == mine) & has_d & (x == RING - 1), OWN, idn),
        ((cu == cd) & has_d, iu, idn),
        ((cz == mine) & has_z, BELOW, OWN),
        ((cz == cu) & has_z & (x > 0), BELOW, iu),
    ]
    flags = jnp.stack([w for w, _, _ in wanted]).astype(jnp.int32)
    order = jnp.cumsum(flags) - 1
    left = jnp.stack([jnp.asarray(i, jnp.int32) for _, i, _ in wanted])
    right = jnp.stack([jnp.asarray(j, jnp.int32) for _, _, j in wanted])
    place = (order[None, :] == jnp.arange(5)[:, None]) & (flags[None, :] == 1)
    left = jnp.sum(jnp.where(place, left[None, :], 0), axis=1)
    right = jnp.sum(jnp.where(place, right[None, :], 0), axis=1)
    pairs = jnp.stack([left, right], axis=1).reshape(-1)
    return jnp.concatenate([jnp.sum(flags)[None], pairs, iu[None], idn[None]]).astype(jnp.int32)


def shards(line, total):
    below_route, first_route, second_route, edge_route, up_route, down_route = routes(total, line)

    def body(embeddings, cluster_sizes):
        normed = unitize(embeddings)
        below = lax.ppermute(normed, AXES, below_route)
        first = lax.ppermute(normed, AXES, first_route)
        second = lax.ppermute(normed, AXES, second_route)
        edge = lax.ppermute(normed, AXES, edge_route)
        own = diag_stats(normed)
        table = pair_table(cluster_sizes, line, total)
        mine, for_up, for_down, for_below = pair_stats(table, normed, first, second, below, edge, own)
        from_down = lax.ppermute(for_down, AXES, inverse(down_route))
        from_up = lax.ppermute(for_up, AXES, inverse(up_route))
        from_below = lax.ppermute(for_below, AXES, inverse(below_route))
        p = lax.axis_index(AXES)
        got_down = p >= 2
        got_below = p < total - RING
        best = jnp.maximum(mine[0], from_up[0])
        best = jnp.maximum(best, jnp.where(got_down, from_down[0], floor_value))
        best = jnp.maximum(best, jnp.where(got_below, from_below[0], floor_value))
        return best, mine[1] + from_up[1] + from_down[1] + from_below[1]

    return body


def solution(mesh):
    line = mesh.shape["blk"]
    total = line * mesh.shape["clus"]
    return jax.shard_map(
        shards(line, total),
        mesh=mesh,
        in_specs=(P(AXES, None), P()),
        out_specs=(P(AXES), P(AXES)),
        check_vma=False,
    )
```

```python
import functools
import math

import jax
import jax.numpy as jnp
from jax import lax
from jax.experimental import pallas as pl
from jax.experimental.pallas import tpu as pltpu
from jax.sharding import PartitionSpec as P

MOST = 5
AXES = ("clus", "blk")
RING = 4

epsilon = 1e-06
threshold = 0.5
sharpness = 20.0
floor_value = -2.0

SLOTS = 5
OWN, FIRST, SECOND, BELOW, EDGE = range(SLOTS)
AT_U, AT_D, USED = 13, 14, 16
TABLE = 32
LANES = 128
TILE = 256


def upper_source(p):
    return p - 1 if p % RING else p + RING - 1


def lower_source(p):
    return p + 1 if p % RING else p + RING + 1


def routes(total, line):
    below, first, second, edge, up, down = [], [], [], [], [], []
    for p in range(total):
        if p >= RING:
            below.append((p - RING, p))
        odd_line = (p // line) % 2
        u, d = upper_source(p), lower_source(p)
        up.append((u, p))
        (second if odd_line else first).append((u, p))
        if d < total:
            down.append((d, p))
            if d // line != p // line:
                edge.append((d, p))
            else:
                (first if odd_line else second).append((d, p))
    return below, first, second, edge, up, down


def inverse(route):
    return [(b, a) for a, b in route]


def unitize(values):
    widened = values.astype(jnp.float32)
    factor = lax.rsqrt(jnp.mean(widened * widened, axis=-1, keepdims=True) + epsilon) * (
        1.0 / math.sqrt(values.shape[-1])
    )
    return (widened * factor).astype(jnp.bfloat16)


def closeness_of(scores):
    return jax.nn.sigmoid(sharpness * (scores - threshold))


def score_block(rows, cols):
    return lax.dot_general(rows, cols, (((1,), (1,)), ((), ())), preferred_element_type=jnp.float32)


def fold_lanes(part, op):
    folded = part[:, :LANES]
    for k in range(1, part.shape[1] // LANES):
        folded = op(folded, part[:, k * LANES : (k + 1) * LANES])
    return folded


def fold_sublanes(part, reduce):
    return reduce(part.reshape(part.shape[0] // 8, 8, part.shape[1]), axis=0)


def write_table(line, total, sizes_ref, place_ref, table_ref):
    p = place_ref[0]
    x = lax.rem(p, RING)
    my_line = lax.div(p, line)
    odd_line = lax.rem(my_line, 2)
    qu = jnp.where(x == 0, p + RING - 1, p - 1)
    qd = jnp.where(x == 0, p + RING + 1, p + 1)
    qz = p - RING

    def step(k, carry):
        end, at_p, at_u, at_d, at_z = carry
        end = end + sizes_ref[k]
        one = jnp.int32(1)
        zero = jnp.int32(0)
        return (
            end,
            at_p + jnp.where(end <= p, one, zero),
            at_u + jnp.where(end <= qu, one, zero),
            at_d + jnp.where(end <= qd, one, zero),
            at_z + jnp.where(end <= qz, one, zero),
        )

    nought = jnp.int32(0)
    _, mine, cu, cd, cz = lax.fori_loop(0, sizes_ref.shape[0], step, (nought,) * 5)
    has_d = qd < total
    has_z = qz >= 0
    iu = jnp.where(odd_line == 1, SECOND, FIRST)
    idn = jnp.where(lax.div(qd, line) != my_line, EDGE, jnp.where(odd_line == 1, FIRST, SECOND))
    wanted = [
        ((cz == mine) & has_z, BELOW, OWN),
        ((cz == cu) & has_z & (x > 0), BELOW, iu),
        (cu == mine, OWN, iu),
        ((cd == mine) & has_d & (x == RING - 1), OWN, idn),
        ((cu == cd) & has_d, iu, idn),
    ]
    n = jnp.int32(0)
    for slot in range(SLOTS):
        table_ref[USED + slot] = 0
    for flag, i, j in wanted:
        table_ref[1 + 2 * n] = jnp.asarray(i, jnp.int32)
        table_ref[2 + 2 * n] = jnp.asarray(j, jnp.int32)
        bit = jnp.where(flag, jnp.int32(1), jnp.int32(0))
        table_ref[USED + i] = jnp.maximum(table_ref[USED + i], bit)
        table_ref[USED + j] = jnp.maximum(table_ref[USED + j], bit)
        n = n + bit
    table_ref[0] = n
    table_ref[AT_U] = jnp.asarray(iu, jnp.int32)
    table_ref[AT_D] = jnp.asarray(idn, jnp.int32)


def diag_kernel(line, total, sizes_ref, place_ref, x_ref, out_ref, table_ref):
    rows = x_ref.shape[0]
    for c in range(rows // TILE):
        span = slice(c * TILE, (c + 1) * TILE)
        scores = score_block(x_ref[...], x_ref[span, :])
        self_pair = lax.broadcasted_iota(jnp.int32, scores.shape, 0) == (
            lax.broadcasted_iota(jnp.int32, scores.shape, 1) + c * TILE
        )
        near = jnp.where(self_pair, 0.0, closeness_of(scores))
        high = jnp.where(self_pair, floor_value, scores)
        out_ref[0:1, span] = jnp.max(high, axis=0, keepdims=True)
        out_ref[1:2, span] = jnp.sum(near, axis=0, keepdims=True)
    write_table(line, total, sizes_ref, place_ref, table_ref)


def pair_kernel(table_ref, own_ref, z_ref, a_ref, b_ref, e_ref, x_ref, ox_ref, ou_ref, od_ref, oz_ref, slabs, best, count, sems):
    held = [(OWN, x_ref), (FIRST, a_ref), (SECOND, b_ref), (BELOW, z_ref), (EDGE, e_ref)]
    rows = slabs.shape[1]
    for slot, ref in held:

        @pl.when(table_ref[USED + slot] == 1)
        def _():
            pltpu.make_async_copy(ref, slabs.at[slot], sems.at[slot]).start()

    best[...] = jnp.full(best.shape, floor_value, jnp.float32)
    count[...] = jnp.zeros(count.shape, jnp.float32)
    for slot, ref in held:

        @pl.when(table_ref[USED + slot] == 1)
        def _():
            pltpu.make_async_copy(ref, slabs.at[slot], sems.at[slot]).wait()

    def one(k, carry):
        i, j = table_ref[2 * k + 1], table_ref[2 * k + 2]
        high_rows = near_rows = None
        for c in range(rows // TILE):
            span = slice(c * TILE, (c + 1) * TILE)
            scores = score_block(slabs[i], slabs[j, span, :])
            near = closeness_of(scores)
            best[j, :, span] = jnp.maximum(best[j, :, span], fold_sublanes(scores, jnp.max))
            count[j, :, span] = count[j, :, span] + fold_sublanes(near, jnp.sum)
            high_part, near_part = fold_lanes(scores, jnp.maximum), fold_lanes(near, jnp.add)
            high_rows = high_part if high_rows is None else jnp.maximum(high_rows, high_part)
            near_rows = near_part if near_rows is None else near_rows + near_part
        best[i] = jnp.maximum(best[i], fold_sublanes(high_rows.T, jnp.max))
        count[i] = count[i] + fold_sublanes(near_rows.T, jnp.sum)
        return carry

    lax.fori_loop(0, table_ref[0], one, 0)

    def emit(ref, slot):
        ref[0:1, :] = jnp.max(best[slot], axis=0, keepdims=True)
        ref[1:2, :] = jnp.sum(count[slot], axis=0, keepdims=True)

    ox_ref[0:1, :] = jnp.maximum(own_ref[0:1, :], jnp.max(best[OWN], axis=0, keepdims=True))
    ox_ref[1:2, :] = own_ref[1:2, :] + jnp.sum(count[OWN], axis=0, keepdims=True)
    emit(ou_ref, table_ref[AT_U])
    emit(od_ref, table_ref[AT_D])
    emit(oz_ref, BELOW)


VMEM = pl.BlockSpec(memory_space=pltpu.VMEM)
SMEM = pl.BlockSpec(memory_space=pltpu.SMEM)
ANY = pl.BlockSpec(memory_space=pl.ANY)


def pair_stats(table, own, below, first, second, edge, own_slab):
    rows, width = own_slab.shape
    stat = jax.ShapeDtypeStruct((2, rows), jnp.float32)
    return pl.pallas_call(
        pair_kernel,
        in_specs=[SMEM, VMEM] + [ANY] * 5,
        out_specs=[VMEM] * 4,
        out_shape=[stat] * 4,
        scratch_shapes=[
            pltpu.VMEM((SLOTS, rows, width), jnp.bfloat16),
            pltpu.VMEM((SLOTS, 8, rows), jnp.float32),
            pltpu.VMEM((SLOTS, 8, rows), jnp.float32),
            pltpu.SemaphoreType.DMA((SLOTS,)),
        ],
        compiler_params=pltpu.CompilerParams(vmem_limit_bytes=24 * 1024 * 1024),
        cost_estimate=pl.CostEstimate(flops=3 * 2 * rows * rows * width, bytes_accessed=5 * rows * width * 2, transcendentals=0),
    )(table, own, below, first, second, edge, own_slab)


def diag_stats(line, total, cluster_sizes, place, own_slab):
    rows, width = own_slab.shape
    return pl.pallas_call(
        functools.partial(diag_kernel, line, total),
        in_specs=[SMEM, SMEM, VMEM],
        out_specs=[VMEM, SMEM],
        out_shape=[
            jax.ShapeDtypeStruct((2, rows), jnp.float32),
            jax.ShapeDtypeStruct((TABLE,), jnp.int32),
        ],
        compiler_params=pltpu.CompilerParams(vmem_limit_bytes=16 * 1024 * 1024),
        cost_estimate=pl.CostEstimate(flops=2 * rows * rows * width, bytes_accessed=rows * width * 2, transcendentals=0),
    )(cluster_sizes, place, own_slab)


def shards(line, total):
    below_route, first_route, second_route, edge_route, up_route, down_route = routes(total, line)

    def body(embeddings, cluster_sizes):
        normed = unitize(embeddings)
        below = lax.ppermute(normed, AXES, below_route)
        first = lax.ppermute(normed, AXES, first_route)
        second = lax.ppermute(normed, AXES, second_route)
        edge = lax.ppermute(normed, AXES, edge_route)
        p = lax.axis_index(AXES)
        own, table = diag_stats(line, total, cluster_sizes, p[None].astype(jnp.int32), normed)
        mine, for_up, for_down, for_below = pair_stats(table, own, below, first, second, edge, normed)
        from_down = lax.ppermute(for_down, AXES, inverse(down_route))
        from_up = lax.ppermute(for_up, AXES, inverse(up_route))
        from_below = lax.ppermute(for_below, AXES, inverse(below_route))
        got_down = p >= 2
        got_below = p < total - RING
        best = jnp.maximum(mine[0], from_up[0])
        best = jnp.maximum(best, jnp.where(got_down, from_down[0], floor_value))
        best = jnp.maximum(best, jnp.where(got_below, from_below[0], floor_value))
        return best, mine[1] + from_up[1] + from_down[1] + from_below[1]

    return body


def solution(mesh):
    line = mesh.shape["blk"]
    total = line * mesh.shape["clus"]
    return jax.shard_map(
        shards(line, total),
        mesh=mesh,
        in_specs=(P(AXES, None), P()),
        out_specs=(P(AXES), P(AXES)),
        check_vma=False,
    )
```

```python
import functools
import math

import jax
import jax.numpy as jnp
from jax import lax
from jax.experimental import pallas as pl
from jax.experimental.pallas import tpu as pltpu
from jax.sharding import PartitionSpec as P

MOST = 5
AXES = ("clus", "blk")
RING = 4

epsilon = 1e-06
threshold = 0.5
sharpness = 20.0
floor_value = -2.0

SLOTS = 3
OWN, UP, THIRD = range(SLOTS)
USED, SEGMENT = 8, 16
TABLE = 2 * SEGMENT
LANES = 128
TILE = 256


def upper_source(p):
    return p - 1 if p % RING else p + RING - 1


def lower_source(p):
    return p + 1 if p % RING else p + RING + 1


def routes(total):
    below, up, down = [], [], []
    for p in range(total):
        if p >= RING:
            below.append((p - RING, p))
        up.append((upper_source(p), p))
        if lower_source(p) < total:
            down.append((lower_source(p), p))
    return below, up, down


def inverse(route):
    return [(b, a) for a, b in route]


def unitize(values):
    widened = values.astype(jnp.float32)
    factor = lax.rsqrt(jnp.mean(widened * widened, axis=-1, keepdims=True) + epsilon) * (
        1.0 / math.sqrt(values.shape[-1])
    )
    return (widened * factor).astype(jnp.bfloat16)


def closeness_of(scores):
    return jax.nn.sigmoid(sharpness * (scores - threshold))


def score_block(rows, cols):
    return lax.dot_general(rows, cols, (((1,), (1,)), ((), ())), preferred_element_type=jnp.float32)


def fold_lanes(part, op):
    folded = part[:, :LANES]
    for k in range(1, part.shape[1] // LANES):
        folded = op(folded, part[:, k * LANES : (k + 1) * LANES])
    return folded


def fold_sublanes(part, reduce):
    return reduce(part.reshape(part.shape[0] // 8, 8, part.shape[1]), axis=0)


def write_table(total, sizes_ref, place_ref, table_ref):
    p = place_ref[0]
    x = lax.rem(p, RING)
    qu = jnp.where(x == 0, p + RING - 1, p - 1)
    qd = jnp.where(x == 0, p + RING + 1, p + 1)
    qz = p - RING

    def step(k, carry):
        end, at_p, at_u, at_d, at_z = carry
        end = end + sizes_ref[k]
        one = jnp.int32(1)
        zero = jnp.int32(0)
        return (
            end,
            at_p + jnp.where(end <= p, one, zero),
            at_u + jnp.where(end <= qu, one, zero),
            at_d + jnp.where(end <= qd, one, zero),
            at_z + jnp.where(end <= qz, one, zero),
        )

    nought = jnp.int32(0)
    _, mine, cu, cd, cz = lax.fori_loop(0, sizes_ref.shape[0], step, (nought,) * 5)
    has_d = qd < total
    has_z = qz >= 0
    parts = [
        [
            (cu == mine, OWN, UP),
            ((cz == mine) & has_z, THIRD, OWN),
            ((cz == cu) & has_z & (x > 0), THIRD, UP),
        ],
        [
            ((cd == mine) & has_d & (x == RING - 1), OWN, THIRD),
            ((cu == cd) & has_d, UP, THIRD),
        ],
    ]
    for part, wanted in enumerate(parts):
        base = part * SEGMENT
        n = nought
        used = [nought] * SLOTS
        for flag, i, j in wanted:
            table_ref[base + 1 + 2 * n] = jnp.int32(i)
            table_ref[base + 2 + 2 * n] = jnp.int32(j)
            bit = jnp.where(flag, jnp.int32(1), nought)
            used[i] = jnp.maximum(used[i], bit)
            used[j] = jnp.maximum(used[j], bit)
            n = n + bit
        table_ref[base] = n
        for slot in range(SLOTS):
            table_ref[base + USED + slot] = used[slot]


def diag_kernel(total, sizes_ref, place_ref, x_ref, out_ref, table_ref):
    rows = x_ref.shape[0]
    for c in range(rows // TILE):
        span = slice(c * TILE, (c + 1) * TILE)
        scores = score_block(x_ref[...], x_ref[span, :])
        self_pair = lax.broadcasted_iota(jnp.int32, scores.shape, 0) == (
            lax.broadcasted_iota(jnp.int32, scores.shape, 1) + c * TILE
        )
        near = jnp.where(self_pair, 0.0, closeness_of(scores))
        high = jnp.where(self_pair, floor_value, scores)
        out_ref[0:1, span] = jnp.max(high, axis=0, keepdims=True)
        out_ref[1:2, span] = jnp.sum(near, axis=0, keepdims=True)
    write_table(total, sizes_ref, place_ref, table_ref)


def pair_kernel(base, table_ref, *refs):
    *held, third_ref, up_ref, own_ref, out_own, out_up, out_third, slabs, best, count, sems = refs
    rows = slabs.shape[1]
    sources = [(OWN, own_ref), (UP, up_ref), (THIRD, third_ref)]
    for slot, ref in sources:

        @pl.when(table_ref[base + USED + slot] == 1)
        def _():
            pltpu.make_async_copy(ref, slabs.at[slot], sems.at[slot]).start()

    best[...] = jnp.full(best.shape, floor_value, jnp.float32)
    count[...] = jnp.zeros(count.shape, jnp.float32)
    for slot, ref in sources:

        @pl.when(table_ref[base + USED + slot] == 1)
        def _():
            pltpu.make_async_copy(ref, slabs.at[slot], sems.at[slot]).wait()

    def one(k, carry):
        i, j = table_ref[base + 2 * k + 1], table_ref[base + 2 * k + 2]
        high_rows = near_rows = None
        for c in range(rows // TILE):
            span = slice(c * TILE, (c + 1) * TILE)
            scores = score_block(slabs[i], slabs[j, span, :])
            near = closeness_of(scores)
            best[j, :, span] = jnp.maximum(best[j, :, span], fold_sublanes(scores, jnp.max))
            count[j, :, span] = count[j, :, span] + fold_sublanes(near, jnp.sum)
            high_part, near_part = fold_lanes(scores, jnp.maximum), fold_lanes(near, jnp.add)
            high_rows = high_part if high_rows is None else jnp.maximum(high_rows, high_part)
            near_rows = near_part if near_rows is None else near_rows + near_part
        best[i] = jnp.maximum(best[i], fold_sublanes(high_rows.T, jnp.max))
        count[i] = count[i] + fold_sublanes(near_rows.T, jnp.sum)
        return carry

    lax.fori_loop(0, table_ref[base], one, 0)

    for slot, ref in enumerate((out_own, out_up, out_third)):
        high = jnp.max(best[slot], axis=0, keepdims=True)
        near = jnp.sum(count[slot], axis=0, keepdims=True)
        if slot < len(held):
            high = jnp.maximum(held[slot][0:1, :], high)
            near = held[slot][1:2, :] + near
        ref[0:1, :] = high
        ref[1:2, :] = near


VMEM = pl.BlockSpec(memory_space=pltpu.VMEM)
SMEM = pl.BlockSpec(memory_space=pltpu.SMEM)
ANY = pl.BlockSpec(memory_space=pl.ANY)


def pair_stats(part, table, held, third, up, own_slab):
    rows, width = own_slab.shape
    stat = jax.ShapeDtypeStruct((2, rows), jnp.float32)
    return pl.pallas_call(
        functools.partial(pair_kernel, part * SEGMENT),
        in_specs=[SMEM] + [VMEM] * len(held) + [ANY] * 3,
        out_specs=[VMEM] * 3,
        out_shape=[stat] * 3,
        scratch_shapes=[
            pltpu.VMEM((SLOTS, rows, width), jnp.bfloat16),
            pltpu.VMEM((SLOTS, 8, rows), jnp.float32),
            pltpu.VMEM((SLOTS, 8, rows), jnp.float32),
            pltpu.SemaphoreType.DMA((SLOTS,)),
        ],
        compiler_params=pltpu.CompilerParams(vmem_limit_bytes=20 * 1024 * 1024),
        cost_estimate=pl.CostEstimate(flops=2 * 2 * rows * rows * width, bytes_accessed=3 * rows * width * 2, transcendentals=0),
    )(table, *held, third, up, own_slab)


def diag_stats(total, cluster_sizes, place, own_slab):
    rows, width = own_slab.shape
    return pl.pallas_call(
        functools.partial(diag_kernel, total),
        in_specs=[SMEM, SMEM, VMEM],
        out_specs=[VMEM, SMEM],
        out_shape=[
            jax.ShapeDtypeStruct((2, rows), jnp.float32),
            jax.ShapeDtypeStruct((TABLE,), jnp.int32),
        ],
        compiler_params=pltpu.CompilerParams(vmem_limit_bytes=16 * 1024 * 1024),
        cost_estimate=pl.CostEstimate(flops=2 * rows * rows * width, bytes_accessed=rows * width * 2, transcendentals=0),
    )(cluster_sizes, place, own_slab)


def shards(total):
    below_route, up_route, down_route = routes(total)

    def body(embeddings, cluster_sizes):
        normed = unitize(embeddings)
        below = lax.ppermute(normed, AXES, below_route)
        up = lax.ppermute(normed, AXES, up_route)
        down = lax.ppermute(normed, AXES, down_route)
        p = lax.axis_index(AXES)
        own, table = diag_stats(total, cluster_sizes, p[None].astype(jnp.int32), normed)
        own, for_up, for_below = pair_stats(0, table, [own], below, up, normed)
        mine, for_up, for_down = pair_stats(1, table, [own, for_up], down, up, normed)
        from_below = lax.ppermute(for_below, AXES, inverse(below_route))
        from_down = lax.ppermute(for_down, AXES, inverse(down_route))
        from_up = lax.ppermute(for_up, AXES, inverse(up_route))
        got_down = p >= 2
        got_below = p < total - RING
        best = jnp.maximum(mine[0], from_up[0])
        best = jnp.maximum(best, jnp.where(got_down, from_down[0], floor_value))
        best = jnp.maximum(best, jnp.where(got_below, from_below[0], floor_value))
        return best, mine[1] + from_up[1] + from_down[1] + from_below[1]

    return body


def solution(mesh):
    total = mesh.shape["blk"] * mesh.shape["clus"]
    return jax.shard_map(
        shards(total),
        mesh=mesh,
        in_specs=(P(AXES, None), P()),
        out_specs=(P(AXES), P(AXES)),
        check_vma=False,
    )
```

```python
import functools
import math

import jax
import jax.numpy as jnp
from jax import lax
from jax.experimental import pallas as pl
from jax.experimental.pallas import tpu as pltpu
from jax.sharding import PartitionSpec as P

MOST = 5
AXES = ("clus", "blk")
RING = 4

epsilon = 1e-06
threshold = 0.5
sharpness = 20.0
floor_value = -2.0

OWN, UP, DOWN, BELOW = range(4)
BELOW_OWN, BELOW_UP, OWN_UP, OWN_UP_LATE, OWN_DOWN, UP_DOWN = range(6)
TABLE = 8
LANES = 128
TILE = 256
CHUNKS = 4


def upper_source(p):
    return p - 1 if p % RING else p + RING - 1


def lower_source(p):
    return p + 1 if p % RING else p + RING + 1


def routes(total):
    below, up, down = [], [], []
    for p in range(total):
        if p >= RING:
            below.append((p - RING, p))
        up.append((upper_source(p), p))
        if lower_source(p) < total:
            down.append((lower_source(p), p))
    return below, up, down


def inverse(route):
    return [(b, a) for a, b in route]


def unitize(values):
    widened = values.astype(jnp.float32)
    factor = lax.rsqrt(jnp.mean(widened * widened, axis=-1, keepdims=True) + epsilon) * (
        1.0 / math.sqrt(values.shape[-1])
    )
    return (widened * factor).astype(jnp.bfloat16)


def closeness_of(scores):
    return jax.nn.sigmoid(sharpness * (scores - threshold))


def score_block(rows, cols):
    return lax.dot_general(rows, cols, (((1,), (1,)), ((), ())), preferred_element_type=jnp.float32)


def fold_lanes(part, op):
    folded = part[:, :LANES]
    for k in range(1, part.shape[1] // LANES):
        folded = op(folded, part[:, k * LANES : (k + 1) * LANES])
    return folded


def fold_sublanes(part, reduce):
    return reduce(part.reshape(part.shape[0] // 8, 8, part.shape[1]), axis=0)


def write_table(total, sizes_ref, place_ref, table_ref):
    p = place_ref[0]
    x = lax.rem(p, RING)
    qu = jnp.where(x == 0, p + RING - 1, p - 1)
    qd = jnp.where(x == 0, p + RING + 1, p + 1)
    qz = p - RING

    def step(k, carry):
        end, at_p, at_u, at_d, at_z = carry
        end = end + sizes_ref[k]
        one = jnp.int32(1)
        zero = jnp.int32(0)
        return (
            end,
            at_p + jnp.where(end <= p, one, zero),
            at_u + jnp.where(end <= qu, one, zero),
            at_d + jnp.where(end <= qd, one, zero),
            at_z + jnp.where(end <= qz, one, zero),
        )

    nought = jnp.int32(0)
    _, mine, cu, cd, cz = lax.fori_loop(0, sizes_ref.shape[0], step, (nought,) * 5)
    has_d = qd < total
    has_z = qz >= 0
    with_up = cu == mine
    below_up = (cz == cu) & has_z & (x > 0)
    flags = {
        BELOW_OWN: (cz == mine) & has_z,
        BELOW_UP: below_up,
        OWN_UP: with_up & ~below_up,
        OWN_UP_LATE: with_up & below_up,
        OWN_DOWN: (cd == mine) & has_d & (x == RING - 1),
        UP_DOWN: (cu == cd) & has_d,
    }
    for place, flag in flags.items():
        table_ref[place] = jnp.where(flag, jnp.int32(1), nought)


def diag_kernel(total, sizes_ref, place_ref, x_ref, out_ref, table_ref):
    rows = x_ref.shape[0]
    for c in range(rows // TILE):
        span = slice(c * TILE, (c + 1) * TILE)
        scores = score_block(x_ref[...], x_ref[span, :])
        self_pair = lax.broadcasted_iota(jnp.int32, scores.shape, 0) == (
            lax.broadcasted_iota(jnp.int32, scores.shape, 1) + c * TILE
        )
        near = jnp.where(self_pair, 0.0, closeness_of(scores))
        high = jnp.where(self_pair, floor_value, scores)
        out_ref[0:1, span] = jnp.max(high, axis=0, keepdims=True)
        out_ref[1:2, span] = jnp.sum(near, axis=0, keepdims=True)
    write_table(total, sizes_ref, place_ref, table_ref)


def pair_kernel(slots, given, pairs, table_ref, *refs):
    n = len(slots)
    held = dict(zip(given, refs))
    slab = dict(zip(slots, refs[len(given) :]))
    out = dict(zip(slots, refs[len(given) + n :]))
    best, count = refs[len(given) + 2 * n :]
    at = {slot: k for k, slot in enumerate(slots)}
    rows = best.shape[2]
    best[...] = jnp.full(best.shape, floor_value, jnp.float32)
    count[...] = jnp.zeros(count.shape, jnp.float32)

    def score_pair(i, j):
        high_rows = near_rows = None
        for c in range(rows // TILE):
            span = slice(c * TILE, (c + 1) * TILE)
            scores = score_block(slab[i][...], slab[j][span, :])
            near = closeness_of(scores)
            best[at[j], :, span] = jnp.maximum(best[at[j], :, span], fold_sublanes(scores, jnp.max))
            count[at[j], :, span] = count[at[j], :, span] + fold_sublanes(near, jnp.sum)
            high_part, near_part = fold_lanes(scores, jnp.maximum), fold_lanes(near, jnp.add)
            high_rows = high_part if high_rows is None else jnp.maximum(high_rows, high_part)
            near_rows = near_part if near_rows is None else near_rows + near_part
        best[at[i]] = jnp.maximum(best[at[i]], fold_sublanes(high_rows.T, jnp.max))
        count[at[i]] = count[at[i]] + fold_sublanes(near_rows.T, jnp.sum)

    for flag, i, j in pairs:
        pl.when(table_ref[flag] == 1)(functools.partial(score_pair, i, j))

    for slot in slots:
        high = jnp.max(best[at[slot]], axis=0, keepdims=True)
        near = jnp.sum(count[at[slot]], axis=0, keepdims=True)
        if slot in held:
            high = jnp.maximum(held[slot][0:1, :], high)
            near = held[slot][1:2, :] + near
        out[slot][0:1, :] = high
        out[slot][1:2, :] = near


def normalise_kernel(x_ref, out_ref, raw, sems):
    rows, width = raw.shape
    step = rows // CHUNKS
    spans = [slice(k * step, (k + 1) * step) for k in range(CHUNKS)]
    copies = [pltpu.make_async_copy(x_ref.at[s, :], raw.at[s, :], sems.at[k]) for k, s in enumerate(spans)]
    for copy in copies:
        copy.start()
    for copy, s in zip(copies, spans):
        copy.wait()
        widened = raw[s, :].astype(jnp.float32)
        mean = jnp.sum(fold_lanes(widened * widened, jnp.add), axis=1, keepdims=True) * (1.0 / width)
        factor = lax.rsqrt(mean + epsilon) * (1.0 / math.sqrt(width))
        out_ref[s, :] = (widened * factor).astype(jnp.bfloat16)


VMEM = pl.BlockSpec(memory_space=pltpu.VMEM)
SMEM = pl.BlockSpec(memory_space=pltpu.SMEM)
ANY = pl.BlockSpec(memory_space=pl.ANY)


def pair_stats(table, stats, slabs, pairs):
    slots, given = list(slabs), list(stats)
    rows, width = slabs[OWN].shape
    outs = pl.pallas_call(
        functools.partial(pair_kernel, slots, given, pairs),
        in_specs=[SMEM] + [VMEM] * (len(given) + len(slots)),
        out_specs=[VMEM] * len(slots),
        out_shape=[jax.ShapeDtypeStruct((2, rows), jnp.float32)] * len(slots),
        scratch_shapes=[pltpu.VMEM((len(slots), 8, rows), jnp.float32)] * 2,
        compiler_params=pltpu.CompilerParams(vmem_limit_bytes=20 * 1024 * 1024),
        cost_estimate=pl.CostEstimate(flops=2 * rows * rows * width, bytes_accessed=len(slots) * rows * width * 2, transcendentals=0),
    )(table, *[stats[s] for s in given], *[slabs[s] for s in slots])
    return dict(zip(slots, outs))


def normalised(embeddings):
    rows, width = embeddings.shape
    return pl.pallas_call(
        normalise_kernel,
        in_specs=[ANY],
        out_specs=VMEM,
        out_shape=jax.ShapeDtypeStruct((rows, width), jnp.bfloat16),
        scratch_shapes=[pltpu.VMEM((rows, width), jnp.bfloat16), pltpu.SemaphoreType.DMA((CHUNKS,))],
        compiler_params=pltpu.CompilerParams(vmem_limit_bytes=16 * 1024 * 1024),
        cost_estimate=pl.CostEstimate(flops=4 * rows * width, bytes_accessed=2 * rows * width * 2, transcendentals=rows),
    )(embeddings)


def diag_stats(total, cluster_sizes, place, own_slab):
    rows, width = own_slab.shape
    return pl.pallas_call(
        functools.partial(diag_kernel, total),
        in_specs=[SMEM, SMEM, VMEM],
        out_specs=[VMEM, SMEM],
        out_shape=[
            jax.ShapeDtypeStruct((2, rows), jnp.float32),
            jax.ShapeDtypeStruct((TABLE,), jnp.int32),
        ],
        compiler_params=pltpu.CompilerParams(vmem_limit_bytes=16 * 1024 * 1024),
        cost_estimate=pl.CostEstimate(flops=2 * rows * rows * width, bytes_accessed=rows * width * 2, transcendentals=0),
    )(cluster_sizes, place, own_slab)


def shards(total):
    below_route, up_route, down_route = routes(total)

    def body(embeddings, cluster_sizes):
        normed = unitize(embeddings)
        below = lax.ppermute(normed, AXES, below_route)
        up = lax.ppermute(normed, AXES, up_route)
        down = lax.ppermute(normed, AXES, down_route)
        p = lax.axis_index(AXES)
        own, table = diag_stats(total, cluster_sizes, p[None].astype(jnp.int32), normed)
        stats = pair_stats(table, {OWN: own}, {BELOW: below, OWN: normed}, [(BELOW_OWN, BELOW, OWN)])
        stats = pair_stats(
            table,
            stats,
            {BELOW: below, UP: up, OWN: normed},
            [(BELOW_UP, BELOW, UP), (OWN_UP, OWN, UP)],
        )
        for_below = stats.pop(BELOW)
        stats = pair_stats(
            table,
            stats,
            {DOWN: down, UP: up, OWN: normed},
            [(OWN_UP_LATE, OWN, UP), (OWN_DOWN, OWN, DOWN), (UP_DOWN, UP, DOWN)],
        )
        mine, for_up, for_down = stats[OWN], stats[UP], stats[DOWN]
        from_below = lax.ppermute(for_below, AXES, inverse(below_route))
        from_down = lax.ppermute(for_down, AXES, inverse(down_route))
        from_up = lax.ppermute(for_up, AXES, inverse(up_route))
        got_down = p >= 2
        got_below = p < total - RING
        best = jnp.maximum(mine[0], from_up[0])
        best = jnp.maximum(best, jnp.where(got_down, from_down[0], floor_value))
        best = jnp.maximum(best, jnp.where(got_below, from_below[0], floor_value))
        return best, mine[1] + from_up[1] + from_down[1] + from_below[1]

    return body


def solution(mesh):
    total = mesh.shape["blk"] * mesh.shape["clus"]
    return jax.shard_map(
        shards(total),
        mesh=mesh,
        in_specs=(P(AXES, None), P()),
        out_specs=(P(AXES), P(AXES)),
        check_vma=False,
    )
```

```python
import functools
import math

import jax
import jax.numpy as jnp
from jax import lax
from jax.experimental import pallas as pl
from jax.experimental.pallas import tpu as pltpu
from jax.sharding import PartitionSpec as P

MOST = 5
AXES = ("clus", "blk")
RING = 4

epsilon = 1e-06
threshold = 0.5
sharpness = 20.0
floor_value = -2.0

OWN, UP, DOWN, BELOW = range(4)
BELOW_OWN, BELOW_UP, OWN_UP, OWN_UP_LATE, OWN_DOWN, UP_DOWN = range(6)
NEEDED = 6
TABLE = 16
LANES = 128
TILE = 256
CHUNKS = 4


def upper_source(p):
    return p - 1 if p % RING else p + RING - 1


def lower_source(p):
    return p + 1 if p % RING else p + RING + 1


def routes(total):
    below, up, down = [], [], []
    for p in range(total):
        if p >= RING:
            below.append((p - RING, p))
        up.append((upper_source(p), p))
        if lower_source(p) < total:
            down.append((lower_source(p), p))
    return below, up, down


def inverse(route):
    return [(b, a) for a, b in route]


def closeness_of(scores):
    return jax.nn.sigmoid(sharpness * (scores - threshold))


def score_block(rows, cols):
    return lax.dot_general(rows, cols, (((1,), (1,)), ((), ())), preferred_element_type=jnp.float32)


def fold_lanes(part, op):
    folded = part[:, :LANES]
    for k in range(1, part.shape[1] // LANES):
        folded = op(folded, part[:, k * LANES : (k + 1) * LANES])
    return folded


def fold_sublanes(part, reduce):
    return reduce(part.reshape(part.shape[0] // 8, 8, part.shape[1]), axis=0)


def normalise(raw_ref, out_ref):
    rows, width = raw_ref.shape
    step = rows // CHUNKS
    for k in range(CHUNKS):
        span = slice(k * step, (k + 1) * step)
        widened = raw_ref[span, :].astype(jnp.float32)
        mean = jnp.sum(fold_lanes(widened * widened, jnp.add), axis=1, keepdims=True) * (1.0 / width)
        factor = lax.rsqrt(mean + epsilon) * (1.0 / math.sqrt(width))
        out_ref[span, :] = (widened * factor).astype(jnp.bfloat16)


def write_table(total, sizes_ref, place_ref, table_ref):
    p = place_ref[0]
    x = lax.rem(p, RING)
    qu = jnp.where(x == 0, p + RING - 1, p - 1)
    qd = jnp.where(x == 0, p + RING + 1, p + 1)
    qz = p - RING

    def step(k, carry):
        end, at_p, at_u, at_d, at_z = carry
        end = end + sizes_ref[k]
        one = jnp.int32(1)
        zero = jnp.int32(0)
        return (
            end,
            at_p + jnp.where(end <= p, one, zero),
            at_u + jnp.where(end <= qu, one, zero),
            at_d + jnp.where(end <= qd, one, zero),
            at_z + jnp.where(end <= qz, one, zero),
        )

    nought = jnp.int32(0)
    _, mine, cu, cd, cz = lax.fori_loop(0, sizes_ref.shape[0], step, (nought,) * 5)
    has_d = qd < total
    has_z = qz >= 0
    with_up = cu == mine
    below_up = (cz == cu) & has_z & (x > 0)
    flags = {
        BELOW_OWN: (cz == mine) & has_z,
        BELOW_UP: below_up,
        OWN_UP: with_up & ~below_up,
        OWN_UP_LATE: with_up & below_up,
        OWN_DOWN: (cd == mine) & has_d & (x == RING - 1),
        UP_DOWN: (cu == cd) & has_d,
    }
    flags[NEEDED + BELOW] = flags[BELOW_OWN] | below_up
    flags[NEEDED + UP] = with_up | below_up | flags[UP_DOWN]
    flags[NEEDED + DOWN] = flags[OWN_DOWN] | flags[UP_DOWN]
    for place, flag in flags.items():
        table_ref[place] = jnp.where(flag, jnp.int32(1), nought)


def diag_kernel(total, sizes_ref, place_ref, raw_ref, out_ref, table_ref, x_ref):
    rows = x_ref.shape[0]
    normalise(raw_ref, x_ref)
    for c in range(rows // TILE):
        span = slice(c * TILE, (c + 1) * TILE)
        scores = score_block(x_ref[...], x_ref[span, :])
        self_pair = lax.broadcasted_iota(jnp.int32, scores.shape, 0) == (
            lax.broadcasted_iota(jnp.int32, scores.shape, 1) + c * TILE
        )
        near = jnp.where(self_pair, 0.0, closeness_of(scores))
        high = jnp.where(self_pair, floor_value, scores)
        out_ref[0:1, span] = jnp.max(high, axis=0, keepdims=True)
        out_ref[1:2, span] = jnp.sum(near, axis=0, keepdims=True)
    write_table(total, sizes_ref, place_ref, table_ref)


def pair_kernel(slots, given, pairs, arrived, table_ref, *refs):
    n = len(slots)
    held = dict(zip(given, refs))
    slab = dict(zip(slots, refs[len(given) :]))
    out = dict(zip(slots, refs[len(given) + n :]))
    ready, best, count = refs[len(given) + 2 * n :]
    raw, slab[arrived] = slab[arrived], ready
    pl.when(table_ref[NEEDED + arrived] == 1)(functools.partial(normalise, raw, ready))
    at = {slot: k for k, slot in enumerate(slots)}
    rows = best.shape[2]
    best[...] = jnp.full(best.shape, floor_value, jnp.float32)
    count[...] = jnp.zeros(count.shape, jnp.float32)

    def score_pair(i, j):
        high_rows = near_rows = None
        for c in range(rows // TILE):
            span = slice(c * TILE, (c + 1) * TILE)
            scores = score_block(slab[i][...], slab[j][span, :])
            near = closeness_of(scores)
            best[at[j], :, span] = jnp.maximum(best[at[j], :, span], fold_sublanes(scores, jnp.max))
            count[at[j], :, span] = count[at[j], :, span] + fold_sublanes(near, jnp.sum)
            high_part, near_part = fold_lanes(scores, jnp.maximum), fold_lanes(near, jnp.add)
            high_rows = high_part if high_rows is None else jnp.maximum(high_rows, high_part)
            near_rows = near_part if near_rows is None else near_rows + near_part
        best[at[i]] = jnp.maximum(best[at[i]], fold_sublanes(high_rows.T, jnp.max))
        count[at[i]] = count[at[i]] + fold_sublanes(near_rows.T, jnp.sum)

    for flag, i, j in pairs:
        pl.when(table_ref[flag] == 1)(functools.partial(score_pair, i, j))

    for slot in slots:
        high = jnp.max(best[at[slot]], axis=0, keepdims=True)
        near = jnp.sum(count[at[slot]], axis=0, keepdims=True)
        if slot in held:
            high = jnp.maximum(held[slot][0:1, :], high)
            near = held[slot][1:2, :] + near
        out[slot][0:1, :] = high
        out[slot][1:2, :] = near


VMEM = pl.BlockSpec(memory_space=pltpu.VMEM)
SMEM = pl.BlockSpec(memory_space=pltpu.SMEM)
ANY = pl.BlockSpec(memory_space=pl.ANY)


def pair_stats(table, stats, slabs, arrived, pairs):
    slots, given = list(slabs), list(stats)
    rows, width = slabs[OWN].shape
    last = arrived == DOWN
    ready = jax.ShapeDtypeStruct((rows, width), jnp.bfloat16)
    kept = [pltpu.VMEM(ready.shape, ready.dtype)] if last else []
    outs = pl.pallas_call(
        functools.partial(pair_kernel, slots, given, pairs, arrived),
        in_specs=[SMEM] + [VMEM] * (len(given) + len(slots)),
        out_specs=[VMEM] * (len(slots) + (not last)),
        out_shape=[jax.ShapeDtypeStruct((2, rows), jnp.float32)] * len(slots) + ([] if last else [ready]),
        scratch_shapes=kept + [pltpu.VMEM((len(slots), 8, rows), jnp.float32)] * 2,
        compiler_params=pltpu.CompilerParams(vmem_limit_bytes=20 * 1024 * 1024),
        cost_estimate=pl.CostEstimate(flops=2 * rows * rows * width, bytes_accessed=len(slots) * rows * width * 2, transcendentals=0),
    )(table, *[stats[s] for s in given], *[slabs[s] for s in slots])
    return dict(zip(slots, outs)), outs[-1]


def diag_stats(total, cluster_sizes, place, own_slab):
    rows, width = own_slab.shape
    return pl.pallas_call(
        functools.partial(diag_kernel, total),
        in_specs=[SMEM, SMEM, VMEM],
        out_specs=[VMEM, SMEM, VMEM],
        out_shape=[
            jax.ShapeDtypeStruct((2, rows), jnp.float32),
            jax.ShapeDtypeStruct((TABLE,), jnp.int32),
            jax.ShapeDtypeStruct((rows, width), jnp.bfloat16),
        ],
        compiler_params=pltpu.CompilerParams(vmem_limit_bytes=16 * 1024 * 1024),
        cost_estimate=pl.CostEstimate(flops=2 * rows * rows * width, bytes_accessed=rows * width * 2, transcendentals=0),
    )(cluster_sizes, place, own_slab)


def shards(total):
    below_route, up_route, down_route = routes(total)

    def body(embeddings, cluster_sizes):
        below = lax.ppermute(embeddings, AXES, below_route)
        up = lax.ppermute(embeddings, AXES, up_route)
        down = lax.ppermute(embeddings, AXES, down_route)
        p = lax.axis_index(AXES)
        own, table, normed = diag_stats(total, cluster_sizes, p[None].astype(jnp.int32), embeddings)
        stats, below = pair_stats(table, {OWN: own}, {BELOW: below, OWN: normed}, BELOW, [(BELOW_OWN, BELOW, OWN)])
        stats, up = pair_stats(
            table,
            stats,
            {BELOW: below, UP: up, OWN: normed},
            UP,
            [(BELOW_UP, BELOW, UP), (OWN_UP, OWN, UP)],
        )
        for_below = stats.pop(BELOW)
        stats, _ = pair_stats(
            table,
            stats,
            {DOWN: down, UP: up, OWN: normed},
            DOWN,
            [(OWN_UP_LATE, OWN, UP), (OWN_DOWN, OWN, DOWN), (UP_DOWN, UP, DOWN)],
        )
        mine, for_up, for_down = stats[OWN], stats[UP], stats[DOWN]
        from_below = lax.ppermute(for_below, AXES, inverse(below_route))
        from_down = lax.ppermute(for_down, AXES, inverse(down_route))
        from_up = lax.ppermute(for_up, AXES, inverse(up_route))
        got_down = p >= 2
        got_below = p < total - RING
        best, count = lax.optimization_barrier(
            (jnp.maximum(mine[0], jnp.where(got_below, from_below[0], floor_value)), mine[1] + from_below[1])
        )
        best = jnp.maximum(best, from_up[0])
        best = jnp.maximum(best, jnp.where(got_down, from_down[0], floor_value))
        return best, count + from_up[1] + from_down[1]

    return body


def solution(mesh):
    total = mesh.shape["blk"] * mesh.shape["clus"]
    return jax.shard_map(
        shards(total),
        mesh=mesh,
        in_specs=(P(AXES, None), P()),
        out_specs=(P(AXES), P(AXES)),
        check_vma=False,
    )
```

```python
import functools
import math

import jax
import jax.numpy as jnp
from jax import lax
from jax.experimental import pallas as pl
from jax.experimental.pallas import tpu as pltpu
from jax.sharding import PartitionSpec as P

MOST = 5
AXES = ("clus", "blk")
RING = 4

epsilon = 1e-06
threshold = 0.5
sharpness = 20.0
floor_value = -2.0

OWN, UP, DOWN, BELOW = range(4)
BELOW_OWN, BELOW_ONLY, BELOW_UP, OWN_UP, UP_ONLY, OWN_UP_LATE, OWN_DOWN, UP_DOWN, BOTH_DOWN = range(9)
MASK = (8, 128)
LANES = 128
TILE = 256
CHUNK = 128


def upper_source(p):
    return p - 1 if p % RING else p + RING - 1


def lower_source(p):
    return p + 1 if p % RING else p + RING + 1


def routes(total):
    below, up, down = [], [], []
    for p in range(total):
        if p >= RING:
            below.append((p - RING, p))
        up.append((upper_source(p), p))
        if lower_source(p) < total:
            down.append((lower_source(p), p))
    return below, up, down


def inverse(route):
    return [(b, a) for a, b in route]


def closeness_of(scores):
    return jax.nn.sigmoid(sharpness * (scores - threshold))


def score_block(rows, cols):
    return lax.dot_general(rows, cols, (((1,), (1,)), ((), ())), preferred_element_type=jnp.float32)


def fold_lanes(part, op):
    folded = part[:, :LANES]
    for k in range(1, part.shape[1] // LANES):
        folded = op(folded, part[:, k * LANES : (k + 1) * LANES])
    return folded


def fold_sublanes(part, reduce):
    return reduce(part.reshape(part.shape[0] // 8, 8, part.shape[1]), axis=0)


def normalise(raw_ref, out_ref, start, stop):
    width = raw_ref.shape[1]
    for k in range(start, stop, CHUNK):
        span = slice(k, k + CHUNK)
        widened = raw_ref[span, :].astype(jnp.float32)
        mean = jnp.sum(fold_lanes(widened * widened, jnp.add), axis=1, keepdims=True) * (1.0 / width)
        factor = lax.rsqrt(mean + epsilon) * (1.0 / math.sqrt(width))
        out_ref[span, :] = (widened * factor).astype(jnp.bfloat16)


def write_mask(total, sizes_ref, place_ref, mask_ref):
    p = place_ref[0]
    x = lax.rem(p, RING)
    qu = jnp.where(x == 0, p + RING - 1, p - 1)
    qd = jnp.where(x == 0, p + RING + 1, p + 1)
    qz = p - RING

    def step(k, carry):
        end, at_p, at_u, at_d, at_z = carry
        end = end + sizes_ref[k]
        one = jnp.int32(1)
        zero = jnp.int32(0)
        return (
            end,
            at_p + jnp.where(end <= p, one, zero),
            at_u + jnp.where(end <= qu, one, zero),
            at_d + jnp.where(end <= qd, one, zero),
            at_z + jnp.where(end <= qz, one, zero),
        )

    nought = jnp.int32(0)
    _, mine, cu, cd, cz = lax.fori_loop(0, sizes_ref.shape[0], step, (nought,) * 5)
    has_d = qd < total
    has_z = qz >= 0
    with_up = cu == mine
    below_up = (cz == cu) & has_z & (x > 0)
    below_own = (cz == mine) & has_z
    own_down = (cd == mine) & has_d & (x == RING - 1)
    up_down = (cu == cd) & has_d
    flags = {
        BELOW_OWN: below_own,
        BELOW_ONLY: below_up & ~below_own,
        BELOW_UP: below_up,
        OWN_UP: with_up & ~below_up,
        UP_ONLY: up_down & ~with_up & ~below_up,
        OWN_UP_LATE: with_up & below_up,
        OWN_DOWN: own_down & ~up_down,
        UP_DOWN: up_down & ~own_down,
        BOTH_DOWN: own_down & up_down,
    }
    bits = nought
    for place, flag in flags.items():
        bits = bits + jnp.where(flag, jnp.int32(1 << place), nought)
    mask_ref[...] = jnp.full(MASK, bits.astype(jnp.float32), jnp.float32)


def diag_kernel(total, sizes_ref, place_ref, raw_ref, out_ref, mask_ref, x_ref):
    rows = x_ref.shape[0]
    normalise(raw_ref, x_ref, 0, rows)
    for c in range(rows // TILE):
        span = slice(c * TILE, (c + 1) * TILE)
        scores = score_block(x_ref[...], x_ref[span, :])
        self_pair = lax.broadcasted_iota(jnp.int32, scores.shape, 0) == (
            lax.broadcasted_iota(jnp.int32, scores.shape, 1) + c * TILE
        )
        near = jnp.where(self_pair, 0.0, closeness_of(scores))
        high = jnp.where(self_pair, floor_value, scores)
        out_ref[0:1, span] = jnp.max(high, axis=0, keepdims=True)
        out_ref[1:2, span] = jnp.sum(near, axis=0, keepdims=True)
    write_mask(total, sizes_ref, place_ref, mask_ref)


def pair_kernel(slots, given, cases, arrived, mask_ref, *refs):
    n = len(slots)
    held = dict(zip(given, refs))
    slab = dict(zip(slots, refs[len(given) :]))
    out = dict(zip(slots, refs[len(given) + n :]))
    ready, best, count = refs[len(given) + 2 * n :]
    raw, slab[arrived] = slab[arrived], ready
    at = {slot: k for k, slot in enumerate(slots)}
    rows = best.shape[2]
    best[...] = jnp.full(best.shape, floor_value, jnp.float32)
    count[...] = jnp.zeros(count.shape, jnp.float32)

    def run(lefts, j):
        high_rows, near_rows = {}, {}
        for start in range(0, rows, TILE):
            span = slice(start, start + TILE)
            if j == arrived:
                normalise(raw, ready, start, start + TILE)
            for i in lefts:
                scores = score_block(slab[i][...], slab[j][span, :])
                near = closeness_of(scores)
                best[at[j], :, span] = jnp.maximum(best[at[j], :, span], fold_sublanes(scores, jnp.max))
                count[at[j], :, span] = count[at[j], :, span] + fold_sublanes(near, jnp.sum)
                high_part, near_part = fold_lanes(scores, jnp.maximum), fold_lanes(near, jnp.add)
                high_rows[i] = high_part if start == 0 else jnp.maximum(high_rows[i], high_part)
                near_rows[i] = near_part if start == 0 else near_rows[i] + near_part
        for i in lefts:
            best[at[i]] = jnp.maximum(best[at[i]], fold_sublanes(high_rows[i].T, jnp.max))
            count[at[i]] = count[at[i]] + fold_sublanes(near_rows[i].T, jnp.sum)

    bits = jnp.max(mask_ref[...]).astype(jnp.int32)
    for flag, lefts, j in cases:
        pl.when((bits & (1 << flag)) != 0)(functools.partial(run, lefts, j))

    for slot in slots:
        high = jnp.max(best[at[slot]], axis=0, keepdims=True)
        near = jnp.sum(count[at[slot]], axis=0, keepdims=True)
        if slot in held:
            high = jnp.maximum(held[slot][0:1, :], high)
            near = held[slot][1:2, :] + near
        out[slot][0:1, :] = high
        out[slot][1:2, :] = near


VMEM = pl.BlockSpec(memory_space=pltpu.VMEM)
SMEM = pl.BlockSpec(memory_space=pltpu.SMEM)
ANY = pl.BlockSpec(memory_space=pl.ANY)


def pair_stats(mask, stats, slabs, arrived, cases):
    slots, given = list(slabs), list(stats)
    rows, width = slabs[OWN].shape
    last = arrived == DOWN
    ready = jax.ShapeDtypeStruct((rows, width), jnp.bfloat16)
    kept = [pltpu.VMEM(ready.shape, ready.dtype)] if last else []
    outs = pl.pallas_call(
        functools.partial(pair_kernel, slots, given, cases, arrived),
        in_specs=[VMEM] * (1 + len(given) + len(slots)),
        out_specs=[VMEM] * (len(slots) + (not last)),
        out_shape=[jax.ShapeDtypeStruct((2, rows), jnp.float32)] * len(slots) + ([] if last else [ready]),
        scratch_shapes=kept + [pltpu.VMEM((len(slots), 8, rows), jnp.float32)] * 2,
        compiler_params=pltpu.CompilerParams(vmem_limit_bytes=20 * 1024 * 1024),
        cost_estimate=pl.CostEstimate(flops=2 * rows * rows * width, bytes_accessed=len(slots) * rows * width * 2, transcendentals=0),
    )(mask, *[stats[s] for s in given], *[slabs[s] for s in slots])
    return dict(zip(slots, outs)), outs[-1]


def diag_stats(total, cluster_sizes, place, own_slab):
    rows, width = own_slab.shape
    return pl.pallas_call(
        functools.partial(diag_kernel, total),
        in_specs=[SMEM, SMEM, VMEM],
        out_specs=[VMEM, VMEM, VMEM],
        out_shape=[
            jax.ShapeDtypeStruct((2, rows), jnp.float32),
            jax.ShapeDtypeStruct(MASK, jnp.float32),
            jax.ShapeDtypeStruct((rows, width), jnp.bfloat16),
        ],
        compiler_params=pltpu.CompilerParams(vmem_limit_bytes=16 * 1024 * 1024),
        cost_estimate=pl.CostEstimate(flops=2 * rows * rows * width, bytes_accessed=rows * width * 2, transcendentals=0),
    )(cluster_sizes, place, own_slab)


def shards(total):
    below_route, up_route, down_route = routes(total)

    def body(embeddings, cluster_sizes):
        below = lax.ppermute(embeddings, AXES, below_route)
        up = lax.ppermute(embeddings, AXES, up_route)
        down = lax.ppermute(embeddings, AXES, down_route)
        p = lax.axis_index(AXES)
        own, mask, normed = diag_stats(total, cluster_sizes, p[None].astype(jnp.int32), embeddings)
        stats, below = pair_stats(
            mask,
            {OWN: own},
            {BELOW: below, OWN: normed},
            BELOW,
            [(BELOW_OWN, (OWN,), BELOW), (BELOW_ONLY, (), BELOW)],
        )
        stats, up = pair_stats(
            mask,
            stats,
            {BELOW: below, UP: up, OWN: normed},
            UP,
            [(BELOW_UP, (BELOW,), UP), (OWN_UP, (OWN,), UP), (UP_ONLY, (), UP)],
        )
        for_below = stats.pop(BELOW)
        stats, _ = pair_stats(
            mask,
            stats,
            {DOWN: down, UP: up, OWN: normed},
            DOWN,
            [
                (OWN_UP_LATE, (OWN,), UP),
                (OWN_DOWN, (OWN,), DOWN),
                (UP_DOWN, (UP,), DOWN),
                (BOTH_DOWN, (OWN, UP), DOWN),
            ],
        )
        mine, for_up, for_down = stats[OWN], stats[UP], stats[DOWN]
        from_below = lax.ppermute(for_below, AXES, inverse(below_route))
        from_down = lax.ppermute(for_down, AXES, inverse(down_route))
        from_up = lax.ppermute(for_up, AXES, inverse(up_route))
        got_down = p >= 2
        got_below = p < total - RING
        best, count = lax.optimization_barrier(
            (jnp.maximum(mine[0], jnp.where(got_below, from_below[0], floor_value)), mine[1] + from_below[1])
        )
        best = jnp.maximum(best, from_up[0])
        best = jnp.maximum(best, jnp.where(got_down, from_down[0], floor_value))
        return best, count + from_up[1] + from_down[1]

    return body


def solution(mesh):
    total = mesh.shape["blk"] * mesh.shape["clus"]
    return jax.shard_map(
        shards(total),
        mesh=mesh,
        in_specs=(P(AXES, None), P()),
        out_specs=(P(AXES), P(AXES)),
        check_vma=False,
    )
```

```python
import functools
import math

import jax
import jax.numpy as jnp
from jax import lax
from jax.experimental import pallas as pl
from jax.experimental.pallas import tpu as pltpu
from jax.sharding import PartitionSpec as P

MOST = 5
AXES = ("clus", "blk")
RING = 4

epsilon = 1e-06
threshold = 0.5
sharpness = 20.0
floor_value = -2.0

OWN, UP, DOWN, BELOW = range(4)
BELOW_OWN, BELOW_ONLY, BELOW_UP, OWN_UP, UP_ONLY, OWN_UP_LATE, OWN_DOWN, UP_DOWN, BOTH_DOWN = range(9)
MASK = (8, 128)
LANES = 128
TILE = 256
CHUNK = 128


def upper_source(p):
    return p - 1 if p % RING else p + RING - 1


def lower_source(p):
    return p + 1 if p % RING else p + RING + 1


def routes(total):
    below, up, down = [], [], []
    for p in range(total):
        if p >= RING:
            below.append((p - RING, p))
        up.append((upper_source(p), p))
        if lower_source(p) < total:
            down.append((lower_source(p), p))
    return below, up, down


def inverse(route):
    return [(b, a) for a, b in route]


def closeness_of(scores):
    return jax.nn.sigmoid(sharpness * (scores - threshold))


def score_block(rows, cols):
    return lax.dot_general(rows, cols, (((1,), (1,)), ((), ())), preferred_element_type=jnp.float32)


def fold_lanes(part, op):
    folded = part[:, :LANES]
    for k in range(1, part.shape[1] // LANES):
        folded = op(folded, part[:, k * LANES : (k + 1) * LANES])
    return folded


def fold_sublanes(part, reduce):
    return reduce(part.reshape(part.shape[0] // 8, 8, part.shape[1]), axis=0)


def normalise(raw_ref, out_ref, start, stop):
    width = raw_ref.shape[1]
    for k in range(start, stop, CHUNK):
        span = slice(k, k + CHUNK)
        widened = raw_ref[span, :].astype(jnp.float32)
        mean = jnp.sum(fold_lanes(widened * widened, jnp.add), axis=1, keepdims=True) * (1.0 / width)
        factor = lax.rsqrt(mean + epsilon) * (1.0 / math.sqrt(width))
        out_ref[span, :] = (widened * factor).astype(jnp.bfloat16)


def write_mask(total, sizes_ref, place_ref, mask_ref):
    p = place_ref[0]
    x = lax.rem(p, RING)
    qu = jnp.where(x == 0, p + RING - 1, p - 1)
    qd = jnp.where(x == 0, p + RING + 1, p + 1)
    qz = p - RING

    def step(k, carry):
        end, at_p, at_u, at_d, at_z = carry
        end = end + sizes_ref[k]
        one = jnp.int32(1)
        zero = jnp.int32(0)
        return (
            end,
            at_p + jnp.where(end <= p, one, zero),
            at_u + jnp.where(end <= qu, one, zero),
            at_d + jnp.where(end <= qd, one, zero),
            at_z + jnp.where(end <= qz, one, zero),
        )

    nought = jnp.int32(0)
    _, mine, cu, cd, cz = lax.fori_loop(0, sizes_ref.shape[0], step, (nought,) * 5)
    has_d = qd < total
    has_z = qz >= 0
    with_up = cu == mine
    below_up = (cz == cu) & has_z & (x > 0)
    below_own = (cz == mine) & has_z
    own_down = (cd == mine) & has_d & (x == RING - 1)
    up_down = (cu == cd) & has_d
    flags = {
        BELOW_OWN: below_own,
        BELOW_ONLY: below_up & ~below_own,
        BELOW_UP: below_up,
        OWN_UP: with_up & ~below_up,
        UP_ONLY: up_down & ~with_up & ~below_up,
        OWN_UP_LATE: with_up & below_up,
        OWN_DOWN: own_down & ~up_down,
        UP_DOWN: up_down & ~own_down,
        BOTH_DOWN: own_down & up_down,
    }
    bits = nought
    for place, flag in flags.items():
        bits = bits + jnp.where(flag, jnp.int32(1 << place), nought)
    mask_ref[...] = jnp.full(MASK, bits.astype(jnp.float32), jnp.float32)


def diag_kernel(total, sizes_ref, place_ref, raw_ref, out_ref, mask_ref, x_ref):
    rows = x_ref.shape[0]
    normalise(raw_ref, x_ref, 0, rows)
    for c in range(rows // TILE):
        span = slice(c * TILE, (c + 1) * TILE)
        scores = score_block(x_ref[...], x_ref[span, :])
        self_pair = lax.broadcasted_iota(jnp.int32, scores.shape, 0) == (
            lax.broadcasted_iota(jnp.int32, scores.shape, 1) + c * TILE
        )
        near = jnp.where(self_pair, 0.0, closeness_of(scores))
        high = jnp.where(self_pair, floor_value, scores)
        out_ref[0:1, span] = jnp.max(high, axis=0, keepdims=True)
        out_ref[1:2, span] = jnp.sum(near, axis=0, keepdims=True)
    write_mask(total, sizes_ref, place_ref, mask_ref)


def pair_kernel(slots, given, cases, arrived, mask_ref, *refs):
    n = len(slots)
    held = dict(zip(given, refs))
    slab = dict(zip(slots, refs[len(given) :]))
    out = dict(zip(slots, refs[len(given) + n :]))
    ready, best, count = refs[len(given) + 2 * n :]
    raw, slab[arrived] = slab[arrived], ready
    at = {slot: k for k, slot in enumerate(slots)}
    rows = best.shape[2]
    best[...] = jnp.full(best.shape, floor_value, jnp.float32)
    count[...] = jnp.zeros(count.shape, jnp.float32)

    def run(lefts, j):
        high_rows, near_rows = {}, {}
        for start in range(0, rows, TILE):
            span = slice(start, start + TILE)
            if j == arrived:
                normalise(raw, ready, start, start + TILE)
            for i in lefts:
                scores = score_block(slab[i][...], slab[j][span, :])
                near = closeness_of(scores)
                high_cols, near_cols = fold_sublanes(scores, jnp.max), fold_sublanes(near, jnp.sum)
                if i != lefts[0]:
                    high_cols = jnp.maximum(best[at[j], :, span], high_cols)
                    near_cols = count[at[j], :, span] + near_cols
                best[at[j], :, span] = high_cols
                count[at[j], :, span] = near_cols
                high_part, near_part = fold_lanes(scores, jnp.maximum), fold_lanes(near, jnp.add)
                high_rows[i] = high_part if start == 0 else jnp.maximum(high_rows[i], high_part)
                near_rows[i] = near_part if start == 0 else near_rows[i] + near_part
        for i in lefts:
            best[at[i]] = fold_sublanes(high_rows[i].T, jnp.max)
            count[at[i]] = fold_sublanes(near_rows[i].T, jnp.sum)

    bits = jnp.max(mask_ref[...]).astype(jnp.int32)
    for flag, lefts, j in cases:
        pl.when((bits & (1 << flag)) != 0)(functools.partial(run, lefts, j))

    for slot in slots:
        high = jnp.max(best[at[slot]], axis=0, keepdims=True)
        near = jnp.sum(count[at[slot]], axis=0, keepdims=True)
        if slot in held:
            high = jnp.maximum(held[slot][0:1, :], high)
            near = held[slot][1:2, :] + near
        out[slot][0:1, :] = high
        out[slot][1:2, :] = near


VMEM = pl.BlockSpec(memory_space=pltpu.VMEM)
SMEM = pl.BlockSpec(memory_space=pltpu.SMEM)
ANY = pl.BlockSpec(memory_space=pl.ANY)


def pair_stats(mask, stats, slabs, arrived, cases):
    slots, given = list(slabs), list(stats)
    rows, width = slabs[OWN].shape
    last = arrived == DOWN
    ready = jax.ShapeDtypeStruct((rows, width), jnp.bfloat16)
    kept = [pltpu.VMEM(ready.shape, ready.dtype)] if last else []
    outs = pl.pallas_call(
        functools.partial(pair_kernel, slots, given, cases, arrived),
        in_specs=[VMEM] * (1 + len(given) + len(slots)),
        out_specs=[VMEM] * (len(slots) + (not last)),
        out_shape=[jax.ShapeDtypeStruct((2, rows), jnp.float32)] * len(slots) + ([] if last else [ready]),
        scratch_shapes=kept + [pltpu.VMEM((len(slots), 8, rows), jnp.float32)] * 2,
        compiler_params=pltpu.CompilerParams(vmem_limit_bytes=20 * 1024 * 1024),
        cost_estimate=pl.CostEstimate(flops=2 * rows * rows * width, bytes_accessed=len(slots) * rows * width * 2, transcendentals=0),
    )(mask, *[stats[s] for s in given], *[slabs[s] for s in slots])
    return dict(zip(slots, outs)), outs[-1]


def diag_stats(total, cluster_sizes, place, own_slab):
    rows, width = own_slab.shape
    return pl.pallas_call(
        functools.partial(diag_kernel, total),
        in_specs=[SMEM, SMEM, VMEM],
        out_specs=[VMEM, VMEM, VMEM],
        out_shape=[
            jax.ShapeDtypeStruct((2, rows), jnp.float32),
            jax.ShapeDtypeStruct(MASK, jnp.float32),
            jax.ShapeDtypeStruct((rows, width), jnp.bfloat16),
        ],
        compiler_params=pltpu.CompilerParams(vmem_limit_bytes=16 * 1024 * 1024),
        cost_estimate=pl.CostEstimate(flops=2 * rows * rows * width, bytes_accessed=rows * width * 2, transcendentals=0),
    )(cluster_sizes, place, own_slab)


def shards(total):
    below_route, up_route, down_route = routes(total)

    def body(embeddings, cluster_sizes):
        below = lax.ppermute(embeddings, AXES, below_route)
        up = lax.ppermute(embeddings, AXES, up_route)
        down = lax.ppermute(embeddings, AXES, down_route)
        p = lax.axis_index(AXES)
        own, mask, normed = diag_stats(total, cluster_sizes, p[None].astype(jnp.int32), embeddings)
        stats, below = pair_stats(
            mask,
            {OWN: own},
            {BELOW: below, OWN: normed},
            BELOW,
            [(BELOW_OWN, (OWN,), BELOW), (BELOW_ONLY, (), BELOW)],
        )
        stats, up = pair_stats(
            mask,
            stats,
            {BELOW: below, UP: up, OWN: normed},
            UP,
            [(BELOW_UP, (BELOW,), UP), (OWN_UP, (OWN,), UP), (UP_ONLY, (), UP)],
        )
        for_below = stats.pop(BELOW)
        stats, _ = pair_stats(
            mask,
            stats,
            {DOWN: down, UP: up, OWN: normed},
            DOWN,
            [
                (OWN_UP_LATE, (OWN,), UP),
                (OWN_DOWN, (OWN,), DOWN),
                (UP_DOWN, (UP,), DOWN),
                (BOTH_DOWN, (OWN, UP), DOWN),
            ],
        )
        mine, for_up, for_down = stats[OWN], stats[UP], stats[DOWN]
        from_below = lax.ppermute(for_below, AXES, inverse(below_route))
        from_down = lax.ppermute(for_down, AXES, inverse(down_route))
        from_up = lax.ppermute(for_up, AXES, inverse(up_route))
        got_down = p >= 2
        got_below = p < total - RING
        best, count = lax.optimization_barrier(
            (jnp.maximum(mine[0], jnp.where(got_below, from_below[0], floor_value)), mine[1] + from_below[1])
        )
        best = jnp.maximum(best, from_up[0])
        best = jnp.maximum(best, jnp.where(got_down, from_down[0], floor_value))
        return best, count + from_up[1] + from_down[1]

    return body


def solution(mesh):
    total = mesh.shape["blk"] * mesh.shape["clus"]
    return jax.shard_map(
        shards(total),
        mesh=mesh,
        in_specs=(P(AXES, None), P()),
        out_specs=(P(AXES), P(AXES)),
        check_vma=False,
    )
```
